32 devices in a mesh: tx: 8 (over y, x, core), ty: 4 (over z).
Axes of the slice: x: 2, y: 2, z: 4, core: 2. Of those that a mesh axis runs over, the one named last changes fastest.
Arguments:
- potential: float32 [8192, 768], P(('tx', 'ty')), may hold values from -3 to 3
- gating: float32 [8192, 768], P(('tx', 'ty')), may hold values from -3 to 3
- ecs_start: float32 [256, 128, 32], P('tx', 'ty'), may hold values from -6 to 6
- templates: bfloat16 [10, 768, 768], replicated, may hold values from -0.21875 to 0.21875
- template_id: int32 [8192], P(('tx', 'ty')), may hold values from 0 to 9
- patch_src: int32 [32768], P(('tx', 'ty')), may hold values from 0 to 3071
- patch_dev: int32 [32768, 1], P(('tx', 'ty')), may hold values from 0 to 31; in each aligned block of 1024 rows (0 to 1023, 1024 to 2047, ...) at most 64 rows name the same one
- patch_dst: int32 [32768], P(('tx', 'ty')), may hold values from 0 to 3071
- patch_conduct: float32 [32768], P(('tx', 'ty')), may hold values from 0.5 to 2
- memb_point: int32 [98304], P(('tx', 'ty')), may hold values from 0 to 32767
Outputs:
- final_potential: float32 [8192, 768], P(('tx', 'ty'))
- final_ecs: float32 [256, 128, 32], P('tx', 'ty')
The draws below stay inside these ranges and needn't reach their ends.
Inputs may be any that keep to these rules, and one draw needn't show every extreme that they name: `patch_dev`: among the 1024 gap junctions listed on one device, at most 64 have their target on any one device, and some device receives exactly 64 from some device.
All inputs are finite; a program needn't handle non-finite values.
Results may differ from the reference program's by a relative error of at most 0.0003.
Values sent between devices are 32-bit elements; how exact they have to be, the bound alone decides.
A program may use at most 128 MiB of HBM per device.

```python
import math
import jax
import jax.numpy as jnp
import numpy as np

NODES = 768
BLOCK = 64
TEMPLATES = 10
CELLS_DEV = 256
P_DEV = 1024
TILE = 32
SWEEPS = 4
STEPS = 2
NCELL = 8192
BLOCKS = 98304
PATCHES = 32768
CAP = 64
NX = 256
NY = 128
N_TY = 4
DEVICES = 32


def with_ends(drawn, key, smallest, top_value):
    extent = drawn.shape
    spot = [jax.random.randint(jax.random.fold_in(key, axis), (), 0, extent[axis]) for axis in range(len(extent))]
    drawn = drawn.at[tuple(spot)].set(smallest)
    longest = extent.index(max(extent))
    spot[longest] = (spot[longest] + 1) % extent[longest]
    return drawn.at[tuple(spot)].set(top_value)


def steps_of(stream_key, shape, cuts, low, top_value):
    def one(dim, parts):
        steps = jax.random.uniform(jax.random.fold_in(jax.random.fold_in(stream_key, 6), dim), (parts,), jnp.float32, low / len(cuts), top_value / len(cuts))
        return jnp.repeat(jnp.exp(steps), shape[dim] // parts).reshape((-1,) + (1,) * (len(shape) - dim - 1))

    level = one(*cuts[0])
    for cut in cuts[1:]:
        level = level * one(*cut)
    return level


def routed_block(own_key, own, number, rows, number_of, top, most, slope):
    order = jax.random.permutation(own_key, number_of)
    packed, ordinary = load_shares(number_of, rows * top, most, slope, True), load_shares(number_of, rows * top, most, slope, False)
    places = jnp.arange(number_of)

    def named(sizes, offset_by):
        used = int((sizes > 0).sum())
        fixed = max(1, used // 4)
        passed = fixed + (places - fixed + offset_by * (used - fixed)) % max(1, number_of - fixed)
        return jnp.zeros((number_of,), jnp.int32).at[order[jnp.where(places < fixed, places, passed)]].set(jnp.asarray(sizes, jnp.int32))

    sizes = jnp.where(number % 4 == 0, named(packed, number // 4), named(ordinary, number - number // 4 - 1))
    mixed = jax.random.permutation(jax.random.fold_in(own, 3), number_of)
    giver, taker = mixed[0:number_of // 2 * 2:2], mixed[1:number_of // 2 * 2:2]
    slack = jnp.minimum(sizes[giver] - 1, most - sizes[taker]) // 2
    slack = jnp.where((giver == order[0]) | (taker == order[0]) | (sizes[taker] == 0), 0, jnp.maximum(slack, 0))
    passed = jax.random.randint(jax.random.fold_in(own, 4), (number_of // 2,), 0, 1 << 20) % (slack + 1)
    sizes = sizes.at[giver].add(-passed).at[taker].add(passed)
    members = jnp.searchsorted(jnp.cumsum(sizes), jnp.arange(rows * top), side="right").astype(jnp.int32)
    listing = members.reshape(top, rows).T
    listing = listing[jax.random.permutation(jax.random.fold_in(own, 1), rows)]
    offset_by = jax.random.randint(jax.random.fold_in(own, 2), (rows, 1), 0, top)
    return jnp.take_along_axis(listing, (jnp.arange(top)[None, :] + offset_by) % top, axis=1)


def load_shares(amount, total, reach, slope, full):
    portions = [(1 << 20) // math.isqrt(grade ** slope) + 1 for grade in range(1, amount + 1)]
    largest = reach if full else min(reach, max(-(-total // amount), total * portions[0] // sum(portions)))
    least = 1 if total - largest >= amount - 1 else 0
    counts, rest = [largest] + [least] * (amount - 1), total - largest - least * (amount - 1)
    while rest > 0:
        movable = [i for i in range(1, amount) if counts[i] < largest] or [i for i in range(1, amount) if counts[i] < reach]
        mass, remaining = sum([portions[i] for i in movable]), rest
        for i in movable:
            extra = min(reach - counts[i], max(1, remaining * portions[i] // mass), rest)
            counts[i] = counts[i] + extra
            rest = rest - extra
    return np.array(counts)


def scatter_about(rng, extent, width, reach, cuts=(), held_as=jnp.bfloat16):
    entries = width * jax.random.normal(rng, extent, jnp.float32)
    if cuts:
        entries = entries * steps_of(rng, extent, cuts, -0.22, 0.18)
    return jnp.clip(entries, -reach, reach).astype(held_as)


def setup_inputs(seed: int = 0) -> dict:
    seeds = jax.random.split(jax.random.key(seed), 11)
    potential = scatter_about(seeds[0], (NCELL, NODES), 1.0, 3.0, ((0, 32),), jnp.float32)
    gating = scatter_about(seeds[1], (NCELL, NODES), 0.5, 3.0, ((0, 32),), jnp.float32)
    ecs_start = scatter_about(seeds[2], (NX, NY, TILE), 1.0, 6.0, ((0, 8), (1, 4)), jnp.float32)
    templates = scatter_about(seeds[3], (TEMPLATES, NODES, NODES), NODES ** -0.5, 0.21875)
    template_id = with_ends(jax.random.randint(seeds[4], (NCELL,), 0, TEMPLATES), jax.random.fold_in(seeds[4], 1), 0, TEMPLATES - 1).astype(jnp.int32)
    patch_src = with_ends(jax.random.randint(seeds[5], (PATCHES,), 0, CELLS_DEV * (NODES // BLOCK)), jax.random.fold_in(seeds[5], 1), 0, (CELLS_DEV * (NODES // BLOCK)) - 1).astype(jnp.int32)
    patch_dev_keys = jax.random.split(jax.random.fold_in(seeds[6], 1), PATCHES // P_DEV)
    patch_dev_turns = jax.random.permutation(jax.random.fold_in(seeds[6], 3), PATCHES // P_DEV)
    patch_dev = jax.vmap(lambda own, number: routed_block(jax.random.fold_in(seeds[6], 2), own, number, P_DEV, DEVICES, 1, CAP, 2))(patch_dev_keys, patch_dev_turns).reshape((PATCHES, 1))
    patch_dst = with_ends(jax.random.randint(seeds[7], (PATCHES,), 0, CELLS_DEV * (NODES // BLOCK)), jax.random.fold_in(seeds[7], 1), 0, (CELLS_DEV * (NODES // BLOCK)) - 1).astype(jnp.int32)
    patch_conduct = jnp.clip(jnp.exp(math.log(2.0) - 1.3862944 * jax.random.uniform(seeds[8], (PATCHES,), jnp.float32) ** steps_of(seeds[8], (PATCHES,), ((0, 32),), -0.2, 0.2)), 0.5, 2.0)
    memb_point = with_ends(jax.random.randint(seeds[9], (BLOCKS,), 0, TILE * TILE * TILE), jax.random.fold_in(seeds[9], 1), 0, (TILE * TILE * TILE) - 1).astype(jnp.int32)
    return {"potential": potential, "gating": gating, "ecs_start": ecs_start, "templates": templates, "template_id": template_id, "patch_src": patch_src, "patch_dev": patch_dev, "patch_dst": patch_dst, "patch_conduct": patch_conduct, "memb_point": memb_point}


def neighbours(phi):
    padded = jnp.pad(phi, 1)
    total = padded[2:, 1:-1, 1:-1] + padded[:-2, 1:-1, 1:-1]
    total = total + padded[1:-1, 2:, 1:-1] + padded[1:-1, :-2, 1:-1]
    return total + padded[1:-1, 1:-1, 2:] + padded[1:-1, 1:-1, :-2]


def reference(potential, gating, ecs_start, templates, template_id, patch_src, patch_dev, patch_dst, patch_conduct, memb_point):
    per_cell = NODES // BLOCK
    dev_blocks = CELLS_DEV * per_cell
    owner = (jnp.arange(PATCHES, dtype=jnp.int32) // P_DEV).astype(jnp.int32)
    source_ids = owner * dev_blocks + patch_src
    target_ids = patch_dev[:, 0] * dev_blocks + patch_dst
    block_ids = jnp.arange(BLOCKS, dtype=jnp.int32)
    device_ids = block_ids // dev_blocks
    grid_x = (device_ids // N_TY) * TILE + memb_point // (TILE * TILE)
    grid_y = (device_ids % N_TY) * TILE + (memb_point // TILE) % TILE
    grid_z = memb_point % TILE
    flat_point = ((grid_x * NY + grid_y) * TILE + grid_z).astype(jnp.int32)
    volt = potential
    recov = gating
    phi = ecs_start
    for step in range(STEPS):
        volt_bf = volt.astype(jnp.bfloat16)
        steklov = jnp.zeros((NCELL, NODES), jnp.float32)
        for index in range(TEMPLATES):
            masked = jnp.where((template_id == index)[:, None], volt_bf, jnp.zeros_like(volt_bf))
            steklov = steklov + jnp.dot(masked, templates[index], preferred_element_type=jnp.float32)
        ion = volt - volt * volt * volt / 3.0 - recov
        blocks = volt.reshape(BLOCKS, BLOCK)
        flux = patch_conduct[:, None] * (blocks[source_ids] - blocks[target_ids])
        gap = jax.ops.segment_sum(flux, target_ids, BLOCKS) - jax.ops.segment_sum(flux, source_ids, BLOCKS)
        current = steklov - ion - gap.reshape(NCELL, NODES)
        block_mean = jnp.mean(current.reshape(BLOCKS, BLOCK), axis=1)
        deposit = jax.ops.segment_sum(block_mean, flat_point, NX * NY * TILE).reshape(NX, NY, TILE)
        for sweep in range(SWEEPS):
            phi = (deposit + neighbours(phi)) / 6.5
        phi_block = phi.reshape(-1)[flat_point]
        phi_nodes = jnp.broadcast_to(phi_block[:, None], (BLOCKS, BLOCK)).reshape(NCELL, NODES)
        recov = recov + 0.05 * 0.08 * (volt + 0.7 - 0.8 * recov)
        volt = volt - 0.05 * (current + phi_nodes)
    return volt, phi
```

```python
import jax
import jax.numpy as jnp
from jax import lax
from jax.sharding import PartitionSpec as P

BLOCK = 64
SWEEPS = 4
STEPS = 2


def extended(x, sides, width):
    for axis, dim in sides:
        devices, length = (lax.axis_size(axis), x.shape[dim])
        up = [(i, (i + 1) % devices) for i in range(devices - 1)]
        down = [(j, i) for i, j in up]
        last = lax.slice_in_dim(x, length - width, length, axis=dim)
        leading = lax.slice_in_dim(x, 0, width, axis=dim)
        before = lax.ppermute(last, axis, up)
        after = lax.ppermute(leading, axis, down)
        x = jnp.concatenate([before, x, after], axis=dim)
    return x


def stencil_sum(framed):
    total = framed[2:, 1:-1, 1:-1] + framed[:-2, 1:-1, 1:-1]
    total = total + framed[1:-1, 2:, 1:-1] + framed[1:-1, :-2, 1:-1]
    return total + framed[1:-1, 1:-1, 2:] + framed[1:-1, 1:-1, :-2]


def on_device(
    potential,
    gating,
    ecs_start,
    templates,
    template_id,
    patch_src,
    patch_dev,
    patch_dst,
    patch_conduct,
    memb_point,
):
    cells = potential.shape[0]
    nodes = potential.shape[1]
    width = BLOCK
    dev_blocks = cells * (nodes // width)
    tile = ecs_start.shape[0]
    count_x = lax.axis_size("tx")
    count_y = lax.axis_size("ty")
    devices = count_x * count_y
    patches = patch_src.shape[0]
    capacity = 2 * patches // devices
    targets = patch_dev[:, 0]
    onehot = (targets[:, None] == jnp.arange(devices, dtype=jnp.int32)[None, :]).astype(jnp.int32)
    order = jnp.arange(patches, dtype=jnp.int32)
    earlier = (order[:, None] > order[None, :]).astype(jnp.bfloat16)
    before = jnp.dot(earlier, onehot.astype(jnp.bfloat16), preferred_element_type=jnp.float32)
    slot = jnp.sum(onehot * before.astype(jnp.int32), axis=1)
    position = targets * capacity + slot
    send_conduct = jnp.zeros((devices * capacity,), jnp.float32).at[position].set(patch_conduct)
    send_target = jnp.full((devices * capacity,), -1, jnp.int32).at[position].set(patch_dst)
    start_x = lax.axis_index("tx") * tile
    start_y = lax.axis_index("ty") * tile
    volt = potential
    recov = gating
    phi = ecs_start
    for step in range(STEPS):
        volt_bf = volt.astype(jnp.bfloat16)
        steklov = jnp.zeros((cells, nodes), jnp.float32)
        for index in range(templates.shape[0]):
            masked = jnp.where((template_id == index)[:, None], volt_bf, jnp.zeros_like(volt_bf))
            steklov = steklov + jnp.dot(
                masked, templates[index], preferred_element_type=jnp.float32
            )
        ion = volt - volt * volt * volt / 3.0 - recov
        blocks = volt.reshape(dev_blocks, width)
        own_source = blocks[patch_src]
        send_volt = jnp.zeros((devices * capacity, width), jnp.float32).at[position].set(own_source)
        got_volt, got_conduct, got_target = (
            lax.all_to_all(
                send_volt.reshape(devices, capacity, width),
                ("tx", "ty"),
                split_axis=0,
                concat_axis=0,
                tiled=True,
            ),
            lax.all_to_all(
                send_conduct.reshape(devices, capacity),
                ("tx", "ty"),
                split_axis=0,
                concat_axis=0,
                tiled=True,
            ),
            lax.all_to_all(
                send_target.reshape(devices, capacity),
                ("tx", "ty"),
                split_axis=0,
                concat_axis=0,
                tiled=True,
            ),
        )
        got_volt = got_volt.reshape(devices * capacity, width)
        got_conduct = got_conduct.reshape(devices * capacity)
        got_target = got_target.reshape(devices * capacity)
        valid = got_target >= 0
        safe_target = jnp.where(valid, got_target, 0)
        flux = got_conduct[:, None] * (got_volt - blocks[safe_target])
        flux = jnp.where(valid[:, None], flux, 0.0)
        gap_in = jax.ops.segment_sum(flux, safe_target, dev_blocks)
        back = lax.all_to_all(
            flux.reshape(devices, capacity, width),
            ("tx", "ty"),
            split_axis=0,
            concat_axis=0,
            tiled=True,
        )
        back = back.reshape(devices * capacity, width)
        gap_out = jax.ops.segment_sum(back[position], patch_src, dev_blocks)
        gap = gap_in - gap_out
        current = steklov - ion - gap.reshape(cells, nodes)
        block_mean = jnp.mean(current.reshape(dev_blocks, width), axis=1)
        deposit = jax.ops.segment_sum(block_mean, memb_point, tile * tile * tile).reshape(
            tile, tile, tile
        )
        depth = SWEEPS
        framed_phi, framed_dep = (
            extended(phi, (("tx", 0), ("ty", 1)), depth),
            extended(deposit, (("tx", 0), ("ty", 1)), depth),
        )
        current_phi = framed_phi
        for sweep in range(SWEEPS):
            rim = depth - sweep - 1
            padded = jnp.pad(current_phi, ((0, 0), (0, 0), (1, 1)))
            total = stencil_sum(padded)
            lo = depth - rim
            hi = depth + tile + rim
            dep_crop = framed_dep[lo:hi, lo:hi, :]
            updated = (dep_crop + total) / 6.5
            span = jnp.arange(tile + 2 * rim, dtype=jnp.int32) - rim
            inside_x = (start_x + span >= 0) & (start_x + span < tile * count_x)
            inside_y = (start_y + span >= 0) & (start_y + span < tile * count_y)
            inside = inside_x[:, None, None] & inside_y[None, :, None]
            current_phi = jnp.where(inside, updated, 0.0)
        phi = current_phi
        phi_block = phi.reshape(-1)[memb_point]
        phi_nodes = jnp.broadcast_to(phi_block[:, None], (dev_blocks, width)).reshape(cells, nodes)
        recov = recov + 0.05 * 0.08 * (volt + 0.7 - 0.8 * recov)
        volt = volt - 0.05 * (current + phi_nodes)
    return (volt, phi)


def solution(mesh):
    return jax.shard_map(
        on_device,
        mesh=mesh,
        in_specs=(
            P(("tx", "ty"), None),
            P(("tx", "ty"), None),
            P("tx", "ty", None),
            P(),
            P(("tx", "ty")),
            P(("tx", "ty")),
            P(("tx", "ty"), None),
            P(("tx", "ty")),
            P(("tx", "ty")),
            P(("tx", "ty")),
        ),
        out_specs=(P(("tx", "ty"), None), P("tx", "ty", None)),
        check_vma=False,
    )
```

```python
import jax
import jax.numpy as jnp
from jax import lax
from jax.experimental import pallas as pl
from jax.experimental.pallas import tpu as pltpu
from jax.sharding import PartitionSpec as P

BLOCK = 64
SWEEPS = 4
STEPS = 2
LANES = 128
VMEM_BYTES = 40 * 1024 * 1024


def extended(x, sides, width):
    for axis, dim in sides:
        devices, length = (lax.axis_size(axis), x.shape[dim])
        up = [(i, (i + 1) % devices) for i in range(devices - 1)]
        down = [(j, i) for i, j in up]
        last = lax.slice_in_dim(x, length - width, length, axis=dim)
        leading = lax.slice_in_dim(x, 0, width, axis=dim)
        before = lax.ppermute(last, axis, up)
        after = lax.ppermute(leading, axis, down)
        x = jnp.concatenate([before, x, after], axis=dim)
    return x


def stencil_sum(framed):
    total = framed[2:, 1:-1, 1:-1] + framed[:-2, 1:-1, 1:-1]
    total = total + framed[1:-1, 2:, 1:-1] + framed[1:-1, :-2, 1:-1]
    return total + framed[1:-1, 1:-1, 2:] + framed[1:-1, 1:-1, :-2]


def two_parts(x):
    high = x.astype(jnp.bfloat16)
    low = (x - high.astype(jnp.float32)).astype(jnp.bfloat16)
    return high, low


def dot32(a, b):
    return jnp.dot(a, b, preferred_element_type=jnp.float32)


def onehot_of(hit):
    return jnp.where(hit, 1.0, 0.0).astype(jnp.bfloat16)


def gather_kernel(volt_ref, cols_ref, out_ref, parts_ref):
    cells, nodes = volt_ref.shape
    rows = out_ref.shape[0]

    @pl.when(pl.program_id(0) == 0)
    def _():
        high, low = two_parts(volt_ref[...])
        parts_ref[0:cells, :] = high
        parts_ref[cells : 2 * cells, :] = low

    lane = lax.broadcasted_iota(jnp.int32, (rows, LANES), 1)
    cell_lane = lax.broadcasted_iota(jnp.int32, (rows, cells), 1)

    def pick(cell, spot):
        hit = onehot_of(cell_lane == cell)
        wide = dot32(jnp.concatenate([hit, hit], axis=1), parts_ref[...])
        pair = lax.shift_right_arithmetic(spot, 1)
        picked = jnp.zeros((rows, LANES), jnp.float32)
        for g in range(nodes // LANES):
            picked = jnp.where(pair == g, wide[:, g * LANES : (g + 1) * LANES], picked)
        return picked

    cols = cols_ref[...]
    spot_a, spot_b = cols[:, 1:2], cols[:, 3:4]
    a = pick(cols[:, 0:1], spot_a)
    b = pick(cols[:, 2:3], spot_b)
    a = jnp.where((spot_a & 1) == 1, pltpu.roll(a, BLOCK, 1), a)
    b = jnp.where((spot_b & 1) == 0, pltpu.roll(b, BLOCK, 1), b)
    out_ref[...] = jnp.where(lane < BLOCK, a, b)


def steklov_kernel(ident_ref, volt_ref, recov_ref, template_ref, out_ref):
    index = pl.program_id(0)
    volt = volt_ref[...]

    @pl.when(index == 0)
    def _():
        out_ref[...] = -(volt - volt * volt * volt / 3.0 - recov_ref[...])

    masked = jnp.where(ident_ref[...] == index, volt, 0.0).astype(jnp.bfloat16)
    out_ref[...] += dot32(masked, template_ref[0])


def scatter_kernel(
    got_ref, sent_ref, cols_ref, conduct_ref, cells_ref, base_ref, memb_ref, memb_t_ref, current_ref, deposit_ref, gap_ref
):
    cells, nodes = base_ref.shape
    rows = got_ref.shape[0]

    @pl.when(pl.program_id(0) == 0)
    def _():
        gap_ref[...] = jnp.zeros_like(gap_ref)

    lane = lax.broadcasted_iota(jnp.int32, (rows, LANES), 1)
    half = jnp.where(lane < BLOCK, 0, 1)
    cols = cols_ref[...]
    conduct = conduct_ref[...]
    scale = jnp.where(lane < BLOCK, conduct[:, 0:1], conduct[:, 1:2])
    flux = scale * (got_ref[...] - pltpu.roll(sent_ref[...], BLOCK, 1))
    turned = pltpu.roll(flux, BLOCK, 1)
    own_row = lax.broadcasted_iota(jnp.int32, (cells, rows), 0)

    def spread(cell_row, spot, home):
        hit = onehot_of(own_row == cell_row)
        side = spot & 1
        placed = jnp.where(half == side, jnp.where(side == home, flux, turned), 0.0)
        pair = lax.shift_right_arithmetic(spot, 1)
        total = []
        for g in range(nodes // LANES):
            high, low = two_parts(jnp.where(pair == g, placed, 0.0))
            total.append(jnp.concatenate([high, low], axis=0))
        return dot32(jnp.concatenate([hit, hit], axis=1), jnp.concatenate(total, axis=1))

    gap_ref[...] += spread(cells_ref[1:2, :], cols[:, 3:4], 0)
    gap_ref[...] += spread(cells_ref[0:1, :], cols[:, 1:2], 1)

    @pl.when(pl.program_id(0) == pl.num_programs(0) - 1)
    def _():
        current = base_ref[...] - gap_ref[...]
        current_ref[...] = current
        grid_rows = deposit_ref.shape[0]
        grid_row = lax.broadcasted_iota(jnp.int32, (grid_rows, cells), 0)
        cell_lane = lax.broadcasted_iota(jnp.int32, (cells, LANES), 1)
        total = jnp.zeros(deposit_ref.shape, jnp.float32)
        for k in range(nodes // BLOCK):
            g = k // 2
            part = current[:, g * LANES : (g + 1) * LANES]
            kept = (cell_lane < BLOCK) if k % 2 == 0 else (cell_lane >= BLOCK)
            mean = jnp.sum(jnp.where(kept, part, 0.0), axis=1, keepdims=True) * (1.0 / BLOCK)
            column = memb_ref[:, k : k + 1] & (LANES - 1)
            high, low = two_parts(jnp.where(cell_lane == column, mean, 0.0))
            hit = onehot_of(grid_row == lax.shift_right_arithmetic(memb_t_ref[k : k + 1, :], 7))
            total = total + dot32(hit, high) + dot32(hit, low)
        deposit_ref[...] = total


def update_kernel(volt_ref, recov_ref, current_ref, phi_ref, memb_ref, volt_out, recov_out):
    cells, nodes = volt_ref.shape
    grid_rows = phi_ref.shape[0]
    high, low = two_parts(phi_ref[...])
    both = jnp.concatenate([high, low], axis=0)
    lane = lax.broadcasted_iota(jnp.int32, (cells, LANES), 1)
    grid_lane = lax.broadcasted_iota(jnp.int32, (cells, grid_rows), 1)

    def value(k):
        memb = memb_ref[:, k : k + 1]
        hit = onehot_of(grid_lane == lax.shift_right_arithmetic(memb, 7))
        row = dot32(jnp.concatenate([hit, hit], axis=1), both)
        return jnp.sum(jnp.where(lane == (memb & (LANES - 1)), row, 0.0), axis=1, keepdims=True)

    for g in range(nodes // LANES):
        phi_nodes = jnp.where(lane < BLOCK, value(2 * g), value(2 * g + 1))
        span = slice(g * LANES, (g + 1) * LANES)
        volt, recov = volt_ref[:, span], recov_ref[:, span]
        recov_out[:, span] = recov + 0.05 * 0.08 * (volt + 0.7 - 0.8 * recov)
        volt_out[:, span] = volt - 0.05 * (current_ref[:, span] + phi_nodes)


def params():
    return pltpu.CompilerParams(vmem_limit_bytes=VMEM_BYTES)


def whole_block(shape):
    return pl.BlockSpec(shape, lambda i: (0,) * len(shape))


def gather(volt, cols, slots, tile):
    cells, nodes = volt.shape
    return pl.pallas_call(
        gather_kernel,
        grid=(slots // tile,),
        in_specs=[whole_block((cells, nodes)), pl.BlockSpec((tile, 4), lambda i: (i, 0))],
        out_specs=pl.BlockSpec((tile, LANES), lambda i: (i, 0)),
        out_shape=jax.ShapeDtypeStruct((slots, LANES), jnp.float32),
        scratch_shapes=[pltpu.VMEM((2 * cells, nodes), jnp.bfloat16)],
        compiler_params=params(),
    )(volt, cols)


def steklov(ident, volt, recov, templates):
    cells, nodes = volt.shape
    count = templates.shape[0]
    return pl.pallas_call(
        steklov_kernel,
        grid=(count,),
        in_specs=[
            whole_block((cells, 1)),
            whole_block((cells, nodes)),
            whole_block((cells, nodes)),
            pl.BlockSpec((1, nodes, nodes), lambda i: (i, 0, 0)),
        ],
        out_specs=whole_block((cells, nodes)),
        out_shape=jax.ShapeDtypeStruct((cells, nodes), jnp.float32),
        compiler_params=params(),
        cost_estimate=pl.CostEstimate(
            flops=2 * count * cells * nodes * nodes, bytes_accessed=2 * count * nodes * nodes, transcendentals=0
        ),
    )(ident, volt, recov, templates)


def scatter(got, sent, cols, conduct, cell_rows, base, memb, memb_t, grid_rows, tile):
    cells, nodes = base.shape
    slots = got.shape[0]
    return pl.pallas_call(
        scatter_kernel,
        grid=(slots // tile,),
        in_specs=[
            pl.BlockSpec((tile, LANES), lambda i: (i, 0)),
            pl.BlockSpec((tile, LANES), lambda i: (i, 0)),
            pl.BlockSpec((tile, 4), lambda i: (i, 0)),
            pl.BlockSpec((tile, 2), lambda i: (i, 0)),
            pl.BlockSpec((2, tile), lambda i: (0, i)),
            whole_block((cells, nodes)),
            whole_block(memb.shape),
            whole_block(memb_t.shape),
        ],
        out_specs=[whole_block((cells, nodes)), whole_block((grid_rows, LANES))],
        out_shape=[
            jax.ShapeDtypeStruct((cells, nodes), jnp.float32),
            jax.ShapeDtypeStruct((grid_rows, LANES), jnp.float32),
        ],
        scratch_shapes=[pltpu.VMEM((cells, nodes), jnp.float32)],
        compiler_params=params(),
    )(got, sent, cols, conduct, cell_rows, base, memb, memb_t)


def update(volt, recov, current, phi, memb):
    return pl.pallas_call(
        update_kernel,
        out_shape=[jax.ShapeDtypeStruct(volt.shape, jnp.float32)] * 2,
        compiler_params=params(),
    )(volt, recov, current, phi, memb)


def slot_table(patch_src, targets, patch_dst, patch_conduct, devices, capacity):
    patches = patch_src.shape[0]
    onehot = (targets[:, None] == jnp.arange(devices, dtype=jnp.int32)[None, :]).astype(jnp.int32)
    order = jnp.arange(patches, dtype=jnp.int32)
    earlier = (order[:, None] > order[None, :]).astype(jnp.bfloat16)
    before = dot32(earlier, onehot.astype(jnp.bfloat16))
    slot = jnp.sum(onehot * before.astype(jnp.int32), axis=1)
    position = targets * capacity + slot
    hit = (jnp.arange(devices * capacity, dtype=jnp.int32)[:, None] == position[None, :]).astype(jnp.bfloat16)
    first = lax.reduce_precision(patch_conduct, 8, 7)
    second = lax.reduce_precision(patch_conduct - first, 8, 7)
    third = patch_conduct - first - second
    values = [patch_src // BLOCK, patch_src % BLOCK, patch_dst // BLOCK, patch_dst % BLOCK]
    values = [v.astype(jnp.bfloat16) for v in values + [jnp.ones_like(patch_src), first, second, third]]
    table = dot32(hit, jnp.stack(values, axis=1))
    empty = table[:, 4] - 1.0
    src = table[:, 0] * BLOCK + table[:, 1] + empty
    dst = table[:, 2] * BLOCK + table[:, 3] + empty
    return src, dst, table[:, 5] + table[:, 6] + table[:, 7]


def exchange(x):
    return lax.all_to_all(x, ("tx", "ty"), split_axis=0, concat_axis=0, tiled=True)


def on_device(
    potential,
    gating,
    ecs_start,
    templates,
    template_id,
    patch_src,
    patch_dev,
    patch_dst,
    patch_conduct,
    memb_point,
):
    cells, nodes = potential.shape
    per_cell = nodes // BLOCK
    tile = ecs_start.shape[0]
    points = ecs_start.size
    count_x = lax.axis_size("tx")
    count_y = lax.axis_size("ty")
    devices = count_x * count_y
    patches = patch_src.shape[0]
    capacity = 2 * patches // devices
    slots = devices * capacity
    rows_at_once = min(512, slots)
    src, dst, conduct = slot_table(patch_src, patch_dev[:, 0], patch_dst, patch_conduct, devices, capacity)
    head = jnp.concatenate([dst.reshape(devices, capacity), conduct.reshape(devices, capacity)], axis=1)
    got_head = exchange(head)
    got_dst = got_head[:, :capacity].reshape(slots)
    got_conduct = got_head[:, capacity:].reshape(slots)
    places = []
    for patch in (src, got_dst):
        patch = patch.astype(jnp.int32)
        places += [jnp.where(patch < 0, -1, patch // per_cell), patch % per_cell]
    cols = jnp.stack(places, axis=1)
    cell_rows = jnp.stack([places[0], places[2]], axis=0)
    conduct_cols = jnp.stack([got_conduct, conduct], axis=1)
    memb = memb_point.reshape(cells, per_cell)
    memb_t = memb.T
    ident = template_id[:, None]
    start_x = lax.axis_index("tx") * tile
    start_y = lax.axis_index("ty") * tile
    volt = potential
    recov = gating
    phi = ecs_start
    for step in range(STEPS):
        sent = gather(volt, cols, slots, rows_at_once)
        got = exchange(sent.reshape(devices, capacity, LANES)).reshape(slots, LANES)
        base = steklov(ident, volt, recov, templates)
        current, deposit = scatter(
            got, sent, cols, conduct_cols, cell_rows, base, memb, memb_t, points // LANES, rows_at_once
        )
        deposit = deposit.reshape(ecs_start.shape)
        depth = SWEEPS
        framed_phi, framed_dep = (
            extended(phi, (("tx", 0), ("ty", 1)), depth),
            extended(deposit, (("tx", 0), ("ty", 1)), depth),
        )
        current_phi = framed_phi
        for sweep in range(SWEEPS):
            rim = depth - sweep - 1
            padded = jnp.pad(current_phi, ((0, 0), (0, 0), (1, 1)))
            total = stencil_sum(padded)
            lo = depth - rim
            hi = depth + tile + rim
            dep_crop = framed_dep[lo:hi, lo:hi, :]
            updated = (dep_crop + total) / 6.5
            span = jnp.arange(tile + 2 * rim, dtype=jnp.int32) - rim
            inside_x = (start_x + span >= 0) & (start_x + span < tile * count_x)
            inside_y = (start_y + span >= 0) & (start_y + span < tile * count_y)
            inside = inside_x[:, None, None] & inside_y[None, :, None]
            current_phi = jnp.where(inside, updated, 0.0)
        phi = current_phi
        volt, recov = update(volt, recov, current, phi.reshape(points // LANES, LANES), memb)
    return (volt, phi)


def solution(mesh):
    return jax.shard_map(
        on_device,
        mesh=mesh,
        in_specs=(
            P(("tx", "ty"), None),
            P(("tx", "ty"), None),
            P("tx", "ty", None),
            P(),
            P(("tx", "ty")),
            P(("tx", "ty")),
            P(("tx", "ty"), None),
            P(("tx", "ty")),
            P(("tx", "ty")),
            P(("tx", "ty")),
        ),
        out_specs=(P(("tx", "ty"), None), P("tx", "ty", None)),
        check_vma=False,
    )
```

```python
import functools

import jax
import jax.numpy as jnp
from jax import lax
from jax.experimental import pallas as pl
from jax.experimental.pallas import tpu as pltpu
from jax.sharding import PartitionSpec as P

BLOCK = 64
SWEEPS = 4
STEPS = 2
LANES = 128
VMEM_BYTES = 40 * 1024 * 1024


def extended(x, sides, width):
    for axis, dim in sides:
        devices, length = (lax.axis_size(axis), x.shape[dim])
        up = [(i, (i + 1) % devices) for i in range(devices - 1)]
        down = [(j, i) for i, j in up]
        last = lax.slice_in_dim(x, length - width, length, axis=dim)
        leading = lax.slice_in_dim(x, 0, width, axis=dim)
        before = lax.ppermute(last, axis, up)
        after = lax.ppermute(leading, axis, down)
        x = jnp.concatenate([before, x, after], axis=dim)
    return x


def stencil_sum(framed):
    total = framed[2:, 1:-1, 1:-1] + framed[:-2, 1:-1, 1:-1]
    total = total + framed[1:-1, 2:, 1:-1] + framed[1:-1, :-2, 1:-1]
    return total + framed[1:-1, 1:-1, 2:] + framed[1:-1, 1:-1, :-2]


def two_parts(x):
    high = x.astype(jnp.bfloat16)
    low = (x - high.astype(jnp.float32)).astype(jnp.bfloat16)
    return high, low


def dot32(a, b):
    return jnp.dot(a, b, preferred_element_type=jnp.float32)


def onehot_of(hit):
    return jnp.where(hit, 1.0, 0.0).astype(jnp.bfloat16)


def gather_kernel(volt_ref, cols_ref, out_ref, parts_ref):
    cells, nodes = volt_ref.shape
    rows = out_ref.shape[0]

    @pl.when(pl.program_id(0) == 0)
    def _():
        high, low = two_parts(volt_ref[...])
        parts_ref[0:cells, :] = high
        parts_ref[cells : 2 * cells, :] = low

    lane = lax.broadcasted_iota(jnp.int32, (rows, LANES), 1)
    cell_lane = lax.broadcasted_iota(jnp.int32, (rows, cells), 1)

    def pick(cell, spot):
        hit = onehot_of(cell_lane == cell)
        wide = dot32(jnp.concatenate([hit, hit], axis=1), parts_ref[...])
        pair = lax.shift_right_arithmetic(spot, 1)
        picked = jnp.zeros((rows, LANES), jnp.float32)
        for g in range(nodes // LANES):
            picked = jnp.where(pair == g, wide[:, g * LANES : (g + 1) * LANES], picked)
        return picked

    cols = cols_ref[...]
    spot_a, spot_b = cols[:, 1:2], cols[:, 3:4]
    a = pick(cols[:, 0:1], spot_a)
    b = pick(cols[:, 2:3], spot_b)
    a = jnp.where((spot_a & 1) == 1, pltpu.roll(a, BLOCK, 1), a)
    b = jnp.where((spot_b & 1) == 0, pltpu.roll(b, BLOCK, 1), b)
    out_ref[...] = jnp.where(lane < BLOCK, a, b)


def steklov_kernel(ident_ref, volt_ref, recov_ref, template_ref, out_ref):
    index = pl.program_id(0)
    volt = volt_ref[...]

    @pl.when(index == 0)
    def _():
        out_ref[...] = -(volt - volt * volt * volt / 3.0 - recov_ref[...])

    masked = jnp.where(ident_ref[...] == index, volt, 0.0).astype(jnp.bfloat16)
    out_ref[...] += dot32(masked, template_ref[0])


def scatter_kernel(
    got_ref,
    sent_ref,
    shift_ref,
    cols_ref,
    conduct_ref,
    cells_ref,
    base_ref,
    volt_ref,
    memb_ref,
    memb_t_ref,
    early_ref,
    deposit_ref,
    gap_ref,
):
    cells, nodes = base_ref.shape
    rows = got_ref.shape[0]

    @pl.when(pl.program_id(0) == 0)
    def _():
        gap_ref[...] = jnp.zeros_like(gap_ref)

    lane = lax.broadcasted_iota(jnp.int32, (rows, LANES), 1)
    half = jnp.where(lane < BLOCK, 0, 1)
    cols = cols_ref[...]
    conduct = conduct_ref[...]
    scale = jnp.where(lane < BLOCK, conduct[:, 0:1], conduct[:, 1:2])
    shift = jnp.where(lane < BLOCK, shift_ref[:, 0:1], shift_ref[:, 1:2])
    flux = scale * (got_ref[...] - pltpu.roll(sent_ref[...], BLOCK, 1) - shift)
    turned = pltpu.roll(flux, BLOCK, 1)
    own_row = lax.broadcasted_iota(jnp.int32, (cells, rows), 0)

    def spread(cell_row, spot, home):
        hit = onehot_of(own_row == cell_row)
        side = spot & 1
        placed = jnp.where(half == side, jnp.where(side == home, flux, turned), 0.0)
        pair = lax.shift_right_arithmetic(spot, 1)
        total = []
        for g in range(nodes // LANES):
            high, low = two_parts(jnp.where(pair == g, placed, 0.0))
            total.append(jnp.concatenate([high, low], axis=0))
        return dot32(jnp.concatenate([hit, hit], axis=1), jnp.concatenate(total, axis=1))

    gap_ref[...] += spread(cells_ref[1:2, :], cols[:, 3:4], 0)
    gap_ref[...] += spread(cells_ref[0:1, :], cols[:, 1:2], 1)

    @pl.when(pl.program_id(0) == pl.num_programs(0) - 1)
    def _():
        current = base_ref[...] - gap_ref[...]
        early_ref[...] = volt_ref[...] - 0.05 * current
        grid_rows = deposit_ref.shape[0]
        grid_row = lax.broadcasted_iota(jnp.int32, (grid_rows, cells), 0)
        cell_lane = lax.broadcasted_iota(jnp.int32, (cells, LANES), 1)
        total = jnp.zeros(deposit_ref.shape, jnp.float32)
        for k in range(nodes // BLOCK):
            g = k // 2
            part = current[:, g * LANES : (g + 1) * LANES]
            kept = (cell_lane < BLOCK) if k % 2 == 0 else (cell_lane >= BLOCK)
            mean = jnp.sum(jnp.where(kept, part, 0.0), axis=1, keepdims=True) * (1.0 / BLOCK)
            column = memb_ref[:, k : k + 1] & (LANES - 1)
            high, low = two_parts(jnp.where(cell_lane == column, mean, 0.0))
            hit = onehot_of(grid_row == lax.shift_right_arithmetic(memb_t_ref[k : k + 1, :], 7))
            total = total + dot32(hit, high) + dot32(hit, low)
        deposit_ref[...] = total


def update_kernel(volt_ref, recov_ref, early_ref, phi_ref, memb_ref, volt_out, recov_out, phi_t_ref):
    cells, nodes = volt_ref.shape
    grid_rows = phi_ref.shape[0]
    high, low = two_parts(phi_ref[...])
    both = jnp.concatenate([high, low], axis=0)
    lane = lax.broadcasted_iota(jnp.int32, (cells, LANES), 1)
    grid_lane = lax.broadcasted_iota(jnp.int32, (cells, grid_rows), 1)

    def value(k):
        memb = memb_ref[:, k : k + 1]
        hit = onehot_of(grid_lane == lax.shift_right_arithmetic(memb, 7))
        row = dot32(jnp.concatenate([hit, hit], axis=1), both)
        return jnp.sum(jnp.where(lane == (memb & (LANES - 1)), row, 0.0), axis=1, keepdims=True)

    table = jnp.zeros((cells, LANES), jnp.float32)
    for g in range(nodes // LANES):
        first, second = value(2 * g), value(2 * g + 1)
        table = jnp.where(lane == 2 * g, first, jnp.where(lane == 2 * g + 1, second, table))
        span = slice(g * LANES, (g + 1) * LANES)
        volt, recov = volt_ref[:, span], recov_ref[:, span]
        recov_out[:, span] = recov + 0.05 * 0.08 * (volt + 0.7 - 0.8 * recov)
        volt_out[:, span] = early_ref[:, span] - 0.05 * jnp.where(lane < BLOCK, first, second)
    phi_t_ref[...] = table.T


def slot_phi_kernel(kept, phi_t_ref, cells_ref, spots_ref, out_ref):
    cells = phi_t_ref.shape[1]
    slots = cells_ref.shape[1]
    high, low = two_parts(phi_t_ref[0:kept, :])
    both = jnp.concatenate([high, low], axis=1)
    row_of = lax.broadcasted_iota(jnp.int32, (cells, slots), 0)
    spot_of = lax.broadcasted_iota(jnp.int32, (kept, slots), 0)
    for part in range(2):
        hit = onehot_of(row_of == cells_ref[part : part + 1, :])
        found = dot32(both, jnp.concatenate([hit, hit], axis=0))
        kept_rows = jnp.where(spot_of == spots_ref[part : part + 1, :], found, 0.0)
        out_ref[part : part + 1, :] = jnp.sum(kept_rows, axis=0, keepdims=True)


def params():
    return pltpu.CompilerParams(vmem_limit_bytes=VMEM_BYTES)


def whole_block(shape):
    return pl.BlockSpec(shape, lambda i: (0,) * len(shape))


def gather(volt, cols, slots, tile):
    cells, nodes = volt.shape
    return pl.pallas_call(
        gather_kernel,
        grid=(slots // tile,),
        in_specs=[whole_block((cells, nodes)), pl.BlockSpec((tile, 4), lambda i: (i, 0))],
        out_specs=pl.BlockSpec((tile, LANES), lambda i: (i, 0)),
        out_shape=jax.ShapeDtypeStruct((slots, LANES), jnp.float32),
        scratch_shapes=[pltpu.VMEM((2 * cells, nodes), jnp.bfloat16)],
        compiler_params=params(),
    )(volt, cols)


def steklov(ident, volt, recov, templates):
    cells, nodes = volt.shape
    count = templates.shape[0]
    return pl.pallas_call(
        steklov_kernel,
        grid=(count,),
        in_specs=[
            whole_block((cells, 1)),
            whole_block((cells, nodes)),
            whole_block((cells, nodes)),
            pl.BlockSpec((1, nodes, nodes), lambda i: (i, 0, 0)),
        ],
        out_specs=whole_block((cells, nodes)),
        out_shape=jax.ShapeDtypeStruct((cells, nodes), jnp.float32),
        compiler_params=pltpu.CompilerParams(vmem_limit_bytes=56 * 1024 * 1024),
        cost_estimate=pl.CostEstimate(
            flops=2 * count * cells * nodes * nodes, bytes_accessed=2 * count * nodes * nodes, transcendentals=0
        ),
    )(ident, volt, recov, templates)


def scatter(got, sent, shift, cols, conduct, cell_rows, base, volt, memb, memb_t, grid_rows, tile):
    cells, nodes = base.shape
    slots = got.shape[0]
    return pl.pallas_call(
        scatter_kernel,
        grid=(slots // tile,),
        in_specs=[
            pl.BlockSpec((tile, LANES), lambda i: (i, 0)),
            pl.BlockSpec((tile, LANES), lambda i: (i, 0)),
            pl.BlockSpec((tile, 2), lambda i: (i, 0)),
            pl.BlockSpec((tile, 4), lambda i: (i, 0)),
            pl.BlockSpec((tile, 2), lambda i: (i, 0)),
            pl.BlockSpec((2, tile), lambda i: (0, i)),
            whole_block((cells, nodes)),
            whole_block((cells, nodes)),
            whole_block(memb.shape),
            whole_block(memb_t.shape),
        ],
        out_specs=[whole_block((cells, nodes)), whole_block((grid_rows, LANES))],
        out_shape=[
            jax.ShapeDtypeStruct((cells, nodes), jnp.float32),
            jax.ShapeDtypeStruct((grid_rows, LANES), jnp.float32),
        ],
        scratch_shapes=[pltpu.VMEM((cells, nodes), jnp.float32)],
        compiler_params=params(),
    )(got, sent, shift, cols, conduct, cell_rows, base, volt, memb, memb_t)


def update(volt, recov, early, phi, memb):
    arrays = [volt.shape, volt.shape, (LANES, volt.shape[0])]
    return pl.pallas_call(
        update_kernel,
        out_shape=[jax.ShapeDtypeStruct(shape, jnp.float32) for shape in arrays],
        compiler_params=params(),
    )(volt, recov, early, phi, memb)


def slot_phi(phi_t, cell_rows, spot_rows, per_cell):
    return pl.pallas_call(
        functools.partial(slot_phi_kernel, -(-per_cell // 16) * 16),
        out_shape=jax.ShapeDtypeStruct(cell_rows.shape, jnp.float32),
        compiler_params=params(),
    )(phi_t, cell_rows, spot_rows)


def slot_table(patch_src, targets, patch_dst, patch_conduct, devices, capacity):
    patches = patch_src.shape[0]
    onehot = (targets[:, None] == jnp.arange(devices, dtype=jnp.int32)[None, :]).astype(jnp.int32)
    order = jnp.arange(patches, dtype=jnp.int32)
    earlier = (order[:, None] > order[None, :]).astype(jnp.bfloat16)
    before = dot32(earlier, onehot.astype(jnp.bfloat16))
    slot = jnp.sum(onehot * before.astype(jnp.int32), axis=1)
    position = targets * capacity + slot
    hit = (jnp.arange(devices * capacity, dtype=jnp.int32)[:, None] == position[None, :]).astype(jnp.bfloat16)
    first = lax.reduce_precision(patch_conduct, 8, 7)
    second = lax.reduce_precision(patch_conduct - first, 8, 7)
    third = patch_conduct - first - second
    values = [patch_src // BLOCK, patch_src % BLOCK, patch_dst // BLOCK, patch_dst % BLOCK]
    values = [v.astype(jnp.bfloat16) for v in values + [jnp.ones_like(patch_src), first, second, third]]
    table = dot32(hit, jnp.stack(values, axis=1))
    empty = table[:, 4] - 1.0
    src = table[:, 0] * BLOCK + table[:, 1] + empty
    dst = table[:, 2] * BLOCK + table[:, 3] + empty
    return src, dst, table[:, 5] + table[:, 6] + table[:, 7]


def exchange(x):
    return lax.all_to_all(x, ("tx", "ty"), split_axis=0, concat_axis=0, tiled=True)


def on_device(
    potential,
    gating,
    ecs_start,
    templates,
    template_id,
    patch_src,
    patch_dev,
    patch_dst,
    patch_conduct,
    memb_point,
):
    cells, nodes = potential.shape
    per_cell = nodes // BLOCK
    tile = ecs_start.shape[0]
    points = ecs_start.size
    count_x = lax.axis_size("tx")
    count_y = lax.axis_size("ty")
    devices = count_x * count_y
    patches = patch_src.shape[0]
    capacity = 2 * patches // devices
    slots = devices * capacity
    rows_at_once = min(512, slots)
    src, dst, conduct = slot_table(patch_src, patch_dev[:, 0], patch_dst, patch_conduct, devices, capacity)
    head = jnp.concatenate([dst.reshape(devices, capacity), conduct.reshape(devices, capacity)], axis=1)
    got_head = exchange(head)
    got_dst = got_head[:, :capacity].reshape(slots)
    got_conduct = got_head[:, capacity:].reshape(slots)
    places = []
    for patch in (src, got_dst):
        patch = patch.astype(jnp.int32)
        places += [jnp.where(patch < 0, -1, patch // per_cell), patch % per_cell]
    cols = jnp.stack(places, axis=1)
    cell_rows = jnp.stack([places[0], places[2]], axis=0)
    spot_rows = jnp.stack([places[1], places[3]], axis=0)
    conduct_cols = jnp.stack([got_conduct, conduct], axis=1)
    memb = memb_point.reshape(cells, per_cell)
    memb_t = memb.T
    ident = template_id[:, None]
    start_x = lax.axis_index("tx") * tile
    start_y = lax.axis_index("ty") * tile
    volt = potential
    recov = gating
    phi = ecs_start
    shift = jnp.zeros((slots, 2), jnp.float32)
    sent = gather(volt, cols, slots, rows_at_once)
    got = exchange(sent.reshape(devices, capacity, LANES)).reshape(slots, LANES)
    for step in range(STEPS):
        base = steklov(ident, volt, recov, templates)
        early, deposit = scatter(
            got, sent, shift, cols, conduct_cols, cell_rows, base, volt, memb, memb_t, points // LANES, rows_at_once
        )
        if step + 1 < STEPS:
            sent = gather(early, cols, slots, rows_at_once)
            got = exchange(sent.reshape(devices, capacity, LANES)).reshape(slots, LANES)
        deposit = deposit.reshape(ecs_start.shape)
        depth = SWEEPS
        framed_phi, framed_dep = (
            extended(phi, (("tx", 0), ("ty", 1)), depth),
            extended(deposit, (("tx", 0), ("ty", 1)), depth),
        )
        current_phi = framed_phi
        for sweep in range(SWEEPS):
            rim = depth - sweep - 1
            padded = jnp.pad(current_phi, ((0, 0), (0, 0), (1, 1)))
            total = stencil_sum(padded)
            lo = depth - rim
            hi = depth + tile + rim
            dep_crop = framed_dep[lo:hi, lo:hi, :]
            updated = (dep_crop + total) / 6.5
            span = jnp.arange(tile + 2 * rim, dtype=jnp.int32) - rim
            inside_x = (start_x + span >= 0) & (start_x + span < tile * count_x)
            inside_y = (start_y + span >= 0) & (start_y + span < tile * count_y)
            inside = inside_x[:, None, None] & inside_y[None, :, None]
            current_phi = jnp.where(inside, updated, 0.0)
        phi = current_phi
        volt, recov, phi_t = update(volt, recov, early, phi.reshape(points // LANES, LANES), memb)
        if step + 1 < STEPS:
            own = slot_phi(phi_t, cell_rows, spot_rows, per_cell).reshape(2, devices, capacity)
            other = exchange(jnp.concatenate([own[0], own[1]], axis=1))
            by_source = (other[:, :capacity] - own[1]).reshape(slots)
            by_target = (other[:, capacity:] - own[0]).reshape(slots)
            shift = 0.05 * jnp.stack([by_source, by_target], axis=1)
    return (volt, phi)


def solution(mesh):
    return jax.shard_map(
        on_device,
        mesh=mesh,
        in_specs=(
            P(("tx", "ty"), None),
            P(("tx", "ty"), None),
            P("tx", "ty", None),
            P(),
            P(("tx", "ty")),
            P(("tx", "ty")),
            P(("tx", "ty"), None),
            P(("tx", "ty")),
            P(("tx", "ty")),
            P(("tx", "ty")),
        ),
        out_specs=(P(("tx", "ty"), None), P("tx", "ty", None)),
        check_vma=False,
    )
```

```python
import functools

import jax
import jax.numpy as jnp
from jax import lax
from jax.experimental import pallas as pl
from jax.experimental.pallas import tpu as pltpu
from jax.sharding import PartitionSpec as P

BLOCK = 64
SWEEPS = 4
STEPS = 2
LANES = 128
VMEM_BYTES = 40 * 1024 * 1024


def extended(x, sides, width):
    for axis, dim in sides:
        devices, length = (lax.axis_size(axis), x.shape[dim])
        up = [(i, (i + 1) % devices) for i in range(devices - 1)]
        down = [(j, i) for i, j in up]
        last = lax.slice_in_dim(x, length - width, length, axis=dim)
        leading = lax.slice_in_dim(x, 0, width, axis=dim)
        before = lax.ppermute(last, axis, up)
        after = lax.ppermute(leading, axis, down)
        x = jnp.concatenate([before, x, after], axis=dim)
    return x


def stencil_sum(framed):
    total = framed[2:, 1:-1, 1:-1] + framed[:-2, 1:-1, 1:-1]
    total = total + framed[1:-1, 2:, 1:-1] + framed[1:-1, :-2, 1:-1]
    return total + framed[1:-1, 1:-1, 2:] + framed[1:-1, 1:-1, :-2]


def two_parts(x):
    high = x.astype(jnp.bfloat16)
    low = (x - high.astype(jnp.float32)).astype(jnp.bfloat16)
    return high, low


def dot32(a, b):
    return jnp.dot(a, b, preferred_element_type=jnp.float32)


def onehot_of(hit):
    return jnp.where(hit, 1.0, 0.0).astype(jnp.bfloat16)


def gather_kernel(volt_ref, cols_ref, out_ref, parts_ref):
    cells, nodes = volt_ref.shape
    rows = out_ref.shape[0]

    @pl.when(pl.program_id(0) == 0)
    def _():
        high, low = two_parts(volt_ref[...])
        parts_ref[0:cells, :] = high
        parts_ref[cells : 2 * cells, :] = low

    lane = lax.broadcasted_iota(jnp.int32, (rows, LANES), 1)
    cell_lane = lax.broadcasted_iota(jnp.int32, (rows, cells), 1)

    def pick(cell, spot):
        hit = onehot_of(cell_lane == cell)
        wide = dot32(jnp.concatenate([hit, hit], axis=1), parts_ref[...])
        pair = lax.shift_right_arithmetic(spot, 1)
        picked = jnp.zeros((rows, LANES), jnp.float32)
        for g in range(nodes // LANES):
            picked = jnp.where(pair == g, wide[:, g * LANES : (g + 1) * LANES], picked)
        return picked

    cols = cols_ref[...]
    spot_a, spot_b = cols[:, 1:2], cols[:, 3:4]
    a = pick(cols[:, 0:1], spot_a)
    b = pick(cols[:, 2:3], spot_b)
    a = jnp.where((spot_a & 1) == 1, pltpu.roll(a, BLOCK, 1), a)
    b = jnp.where((spot_b & 1) == 0, pltpu.roll(b, BLOCK, 1), b)
    out_ref[...] = jnp.where(lane < BLOCK, a, b)


def steklov_kernel(ident_ref, volt_ref, recov_ref, template_ref, out_ref):
    index = pl.program_id(0)
    volt = volt_ref[...]

    @pl.when(index == 0)
    def _():
        out_ref[...] = -(volt - volt * volt * volt / 3.0 - recov_ref[...])

    masked = jnp.where(ident_ref[...] == index, volt, 0.0).astype(jnp.bfloat16)
    out_ref[...] += dot32(masked, template_ref[0])


def scatter_kernel(
    got_ref,
    sent_ref,
    shift_ref,
    cols_ref,
    conduct_ref,
    cells_ref,
    base_ref,
    volt_ref,
    memb_ref,
    memb_t_ref,
    early_ref,
    deposit_ref,
    gap_ref,
):
    cells, nodes = base_ref.shape
    rows = got_ref.shape[0]

    @pl.when(pl.program_id(0) == 0)
    def _():
        gap_ref[...] = jnp.zeros_like(gap_ref)

    lane = lax.broadcasted_iota(jnp.int32, (rows, LANES), 1)
    half = jnp.where(lane < BLOCK, 0, 1)
    cols = cols_ref[...]
    conduct = conduct_ref[...]
    scale = jnp.where(lane < BLOCK, conduct[:, 0:1], conduct[:, 1:2])
    shift = jnp.where(lane < BLOCK, shift_ref[:, 0:1], shift_ref[:, 1:2])
    flux = scale * (got_ref[...] - pltpu.roll(sent_ref[...], BLOCK, 1) - shift)
    turned = pltpu.roll(flux, BLOCK, 1)
    own_row = lax.broadcasted_iota(jnp.int32, (cells, rows), 0)

    def spread(cell_row, spot, home):
        hit = onehot_of(own_row == cell_row)
        side = spot & 1
        placed = jnp.where(half == side, jnp.where(side == home, flux, turned), 0.0)
        pair = lax.shift_right_arithmetic(spot, 1)
        total = []
        for g in range(nodes // LANES):
            high, low = two_parts(jnp.where(pair == g, placed, 0.0))
            total.append(jnp.concatenate([high, low], axis=0))
        return dot32(jnp.concatenate([hit, hit], axis=1), jnp.concatenate(total, axis=1))

    gap_ref[...] += spread(cells_ref[1:2, :], cols[:, 3:4], 0)
    gap_ref[...] += spread(cells_ref[0:1, :], cols[:, 1:2], 1)

    @pl.when(pl.program_id(0) == pl.num_programs(0) - 1)
    def _():
        current = base_ref[...] - gap_ref[...]
        early_ref[...] = volt_ref[...] - 0.05 * current
        grid_rows = deposit_ref.shape[0]
        grid_row = lax.broadcasted_iota(jnp.int32, (grid_rows, cells), 0)
        cell_lane = lax.broadcasted_iota(jnp.int32, (cells, LANES), 1)
        total = jnp.zeros(deposit_ref.shape, jnp.float32)
        for k in range(nodes // BLOCK):
            g = k // 2
            part = current[:, g * LANES : (g + 1) * LANES]
            kept = (cell_lane < BLOCK) if k % 2 == 0 else (cell_lane >= BLOCK)
            mean = jnp.sum(jnp.where(kept, part, 0.0), axis=1, keepdims=True) * (1.0 / BLOCK)
            column = memb_ref[:, k : k + 1] & (LANES - 1)
            high, low = two_parts(jnp.where(cell_lane == column, mean, 0.0))
            hit = onehot_of(grid_row == lax.shift_right_arithmetic(memb_t_ref[k : k + 1, :], 7))
            total = total + dot32(hit, high) + dot32(hit, low)
        deposit_ref[...] = total


def update_kernel(volt_ref, recov_ref, early_ref, phi_ref, memb_ref, volt_out, recov_out, phi_t_ref):
    cells, nodes = volt_ref.shape
    grid_rows = phi_ref.shape[0]
    high, low = two_parts(phi_ref[...])
    both = jnp.concatenate([high, low], axis=0)
    lane = lax.broadcasted_iota(jnp.int32, (cells, LANES), 1)
    grid_lane = lax.broadcasted_iota(jnp.int32, (cells, grid_rows), 1)

    def value(k):
        memb = memb_ref[:, k : k + 1]
        hit = onehot_of(grid_lane == lax.shift_right_arithmetic(memb, 7))
        row = dot32(jnp.concatenate([hit, hit], axis=1), both)
        return jnp.sum(jnp.where(lane == (memb & (LANES - 1)), row, 0.0), axis=1, keepdims=True)

    table = jnp.zeros((cells, LANES), jnp.float32)
    for g in range(nodes // LANES):
        first, second = value(2 * g), value(2 * g + 1)
        table = jnp.where(lane == 2 * g, first, jnp.where(lane == 2 * g + 1, second, table))
        span = slice(g * LANES, (g + 1) * LANES)
        volt, recov = volt_ref[:, span], recov_ref[:, span]
        recov_out[:, span] = recov + 0.05 * 0.08 * (volt + 0.7 - 0.8 * recov)
        volt_out[:, span] = early_ref[:, span] - 0.05 * jnp.where(lane < BLOCK, first, second)
    phi_t_ref[...] = table.T


def slot_phi_kernel(kept, phi_t_ref, cells_ref, spots_ref, out_ref):
    cells = phi_t_ref.shape[1]
    slots = cells_ref.shape[1]
    high, low = two_parts(phi_t_ref[0:kept, :])
    both = jnp.concatenate([high, low], axis=1)
    row_of = lax.broadcasted_iota(jnp.int32, (cells, slots), 0)
    spot_of = lax.broadcasted_iota(jnp.int32, (kept, slots), 0)
    for part in range(2):
        hit = onehot_of(row_of == cells_ref[part : part + 1, :])
        found = dot32(both, jnp.concatenate([hit, hit], axis=0))
        kept_rows = jnp.where(spot_of == spots_ref[part : part + 1, :], found, 0.0)
        out_ref[part : part + 1, :] = jnp.sum(kept_rows, axis=0, keepdims=True)


def params():
    return pltpu.CompilerParams(vmem_limit_bytes=VMEM_BYTES)


def whole_block(shape):
    return pl.BlockSpec(shape, lambda i: (0,) * len(shape))


def gather(volt, cols, slots, tile):
    cells, nodes = volt.shape
    return pl.pallas_call(
        gather_kernel,
        grid=(slots // tile,),
        in_specs=[whole_block((cells, nodes)), pl.BlockSpec((tile, 4), lambda i: (i, 0))],
        out_specs=pl.BlockSpec((tile, LANES), lambda i: (i, 0)),
        out_shape=jax.ShapeDtypeStruct((slots, LANES), jnp.float32),
        scratch_shapes=[pltpu.VMEM((2 * cells, nodes), jnp.bfloat16)],
        compiler_params=params(),
    )(volt, cols)


def steklov(ident, volt, recov, templates):
    cells, nodes = volt.shape
    count = templates.shape[0]
    return pl.pallas_call(
        steklov_kernel,
        grid=(count,),
        in_specs=[
            whole_block((cells, 1)),
            whole_block((cells, nodes)),
            whole_block((cells, nodes)),
            pl.BlockSpec((1, nodes, nodes), lambda i: (i, 0, 0)),
        ],
        out_specs=whole_block((cells, nodes)),
        out_shape=jax.ShapeDtypeStruct((cells, nodes), jnp.float32),
        compiler_params=params(),
        cost_estimate=pl.CostEstimate(
            flops=2 * count * cells * nodes * nodes, bytes_accessed=2 * count * nodes * nodes, transcendentals=0
        ),
    )(ident, volt, recov, templates)


def scatter(got, sent, shift, cols, conduct, cell_rows, base, volt, memb, memb_t, grid_rows, tile):
    cells, nodes = base.shape
    slots = got.shape[0]
    return pl.pallas_call(
        scatter_kernel,
        grid=(slots // tile,),
        in_specs=[
            pl.BlockSpec((tile, LANES), lambda i: (i, 0)),
            pl.BlockSpec((tile, LANES), lambda i: (i, 0)),
            pl.BlockSpec((tile, 2), lambda i: (i, 0)),
            pl.BlockSpec((tile, 4), lambda i: (i, 0)),
            pl.BlockSpec((tile, 2), lambda i: (i, 0)),
            pl.BlockSpec((2, tile), lambda i: (0, i)),
            whole_block((cells, nodes)),
            whole_block((cells, nodes)),
            whole_block(memb.shape),
            whole_block(memb_t.shape),
        ],
        out_specs=[whole_block((cells, nodes)), whole_block((grid_rows, LANES))],
        out_shape=[
            jax.ShapeDtypeStruct((cells, nodes), jnp.float32),
            jax.ShapeDtypeStruct((grid_rows, LANES), jnp.float32),
        ],
        scratch_shapes=[pltpu.VMEM((cells, nodes), jnp.float32)],
        compiler_params=params(),
    )(got, sent, shift, cols, conduct, cell_rows, base, volt, memb, memb_t)


def update(volt, recov, early, phi, memb):
    arrays = [volt.shape, volt.shape, (LANES, volt.shape[0])]
    return pl.pallas_call(
        update_kernel,
        out_shape=[jax.ShapeDtypeStruct(shape, jnp.float32) for shape in arrays],
        compiler_params=params(),
    )(volt, recov, early, phi, memb)


def slot_phi(phi_t, cell_rows, spot_rows, per_cell):
    return pl.pallas_call(
        functools.partial(slot_phi_kernel, -(-per_cell // 16) * 16),
        out_shape=jax.ShapeDtypeStruct(cell_rows.shape, jnp.float32),
        compiler_params=params(),
    )(phi_t, cell_rows, spot_rows)


def slot_table(patch_src, targets, patch_dst, patch_conduct, devices, capacity):
    patches = patch_src.shape[0]
    onehot = (targets[:, None] == jnp.arange(devices, dtype=jnp.int32)[None, :]).astype(jnp.int32)
    order = jnp.arange(patches, dtype=jnp.int32)
    earlier = (order[:, None] > order[None, :]).astype(jnp.bfloat16)
    before = dot32(earlier, onehot.astype(jnp.bfloat16))
    slot = jnp.sum(onehot * before.astype(jnp.int32), axis=1)
    position = targets * capacity + slot
    hit = (jnp.arange(devices * capacity, dtype=jnp.int32)[:, None] == position[None, :]).astype(jnp.bfloat16)
    first = lax.reduce_precision(patch_conduct, 8, 7)
    second = lax.reduce_precision(patch_conduct - first, 8, 7)
    third = patch_conduct - first - second
    values = [patch_src // BLOCK, patch_src % BLOCK, patch_dst // BLOCK, patch_dst % BLOCK]
    values = [v.astype(jnp.bfloat16) for v in values + [jnp.ones_like(patch_src), first, second, third]]
    table = dot32(hit, jnp.stack(values, axis=1))
    empty = table[:, 4] - 1.0
    src = table[:, 0] * BLOCK + table[:, 1] + empty
    dst = table[:, 2] * BLOCK + table[:, 3] + empty
    return src, dst, table[:, 5] + table[:, 6] + table[:, 7]


def exchange(x):
    return lax.all_to_all(x, ("tx", "ty"), split_axis=0, concat_axis=0, tiled=True)


def on_device(
    potential,
    gating,
    ecs_start,
    templates,
    template_id,
    patch_src,
    patch_dev,
    patch_dst,
    patch_conduct,
    memb_point,
):
    cells, nodes = potential.shape
    per_cell = nodes // BLOCK
    tile = ecs_start.shape[0]
    points = ecs_start.size
    count_x = lax.axis_size("tx")
    count_y = lax.axis_size("ty")
    devices = count_x * count_y
    patches = patch_src.shape[0]
    capacity = 2 * patches // devices
    slots = devices * capacity
    rows_at_once = min(512, slots)
    src, dst, conduct = slot_table(patch_src, patch_dev[:, 0], patch_dst, patch_conduct, devices, capacity)
    head = jnp.concatenate([dst.reshape(devices, capacity), conduct.reshape(devices, capacity)], axis=1)
    got_head = exchange(head)
    got_dst = got_head[:, :capacity].reshape(slots)
    got_conduct = got_head[:, capacity:].reshape(slots)
    places = []
    for patch in (src, got_dst):
        patch = patch.astype(jnp.int32)
        places += [jnp.where(patch < 0, -1, patch // per_cell), patch % per_cell]
    cols = jnp.stack(places, axis=1)
    cell_rows = jnp.stack([places[0], places[2]], axis=0)
    spot_rows = jnp.stack([places[1], places[3]], axis=0)
    conduct_cols = jnp.stack([got_conduct, conduct], axis=1)
    memb = memb_point.reshape(cells, per_cell)
    memb_t = memb.T
    ident = template_id[:, None]
    start_x = lax.axis_index("tx") * tile
    start_y = lax.axis_index("ty") * tile
    volt = potential
    recov = gating
    phi = ecs_start
    shift = jnp.zeros((slots, 2), jnp.float32)
    sent = gather(volt, cols, slots, rows_at_once)
    got = exchange(sent.reshape(devices, capacity, LANES)).reshape(slots, LANES)
    for step in range(STEPS):
        base = steklov(ident, volt, recov, templates)
        early, deposit = scatter(
            got, sent, shift, cols, conduct_cols, cell_rows, base, volt, memb, memb_t, points // LANES, rows_at_once
        )
        if step + 1 < STEPS:
            sent = gather(early, cols, slots, rows_at_once)
            deposit, sent = lax.optimization_barrier((deposit, sent))
            got = exchange(sent.reshape(devices, capacity, LANES)).reshape(slots, LANES)
        deposit = deposit.reshape(ecs_start.shape)
        depth = SWEEPS
        framed_phi, framed_dep = (
            extended(phi, (("tx", 0), ("ty", 1)), depth),
            extended(deposit, (("tx", 0), ("ty", 1)), depth),
        )
        current_phi = framed_phi
        for sweep in range(SWEEPS):
            rim = depth - sweep - 1
            padded = jnp.pad(current_phi, ((0, 0), (0, 0), (1, 1)))
            total = stencil_sum(padded)
            lo = depth - rim
            hi = depth + tile + rim
            dep_crop = framed_dep[lo:hi, lo:hi, :]
            updated = (dep_crop + total) / 6.5
            span = jnp.arange(tile + 2 * rim, dtype=jnp.int32) - rim
            inside_x = (start_x + span >= 0) & (start_x + span < tile * count_x)
            inside_y = (start_y + span >= 0) & (start_y + span < tile * count_y)
            inside = inside_x[:, None, None] & inside_y[None, :, None]
            current_phi = jnp.where(inside, updated, 0.0)
        phi = current_phi
        volt, recov, phi_t = update(volt, recov, early, phi.reshape(points // LANES, LANES), memb)
        if step + 1 < STEPS:
            own = slot_phi(phi_t, cell_rows, spot_rows, per_cell).reshape(2, devices, capacity)
            own, got = lax.optimization_barrier((own, got))
            other = exchange(jnp.concatenate([own[0], own[1]], axis=1))
            by_source = (other[:, :capacity] - own[1]).reshape(slots)
            by_target = (other[:, capacity:] - own[0]).reshape(slots)
            shift = 0.05 * jnp.stack([by_source, by_target], axis=1)
    return (volt, phi)


def solution(mesh):
    return jax.shard_map(
        on_device,
        mesh=mesh,
        in_specs=(
            P(("tx", "ty"), None),
            P(("tx", "ty"), None),
            P("tx", "ty", None),
            P(),
            P(("tx", "ty")),
            P(("tx", "ty")),
            P(("tx", "ty"), None),
            P(("tx", "ty")),
            P(("tx", "ty")),
            P(("tx", "ty")),
        ),
        out_specs=(P(("tx", "ty"), None), P("tx", "ty", None)),
        check_vma=False,
    )
```

```python
import jax
import jax.numpy as jnp
from jax import lax
from jax.experimental import pallas as pl
from jax.experimental.pallas import tpu as pltpu
from jax.sharding import PartitionSpec as P

BLOCK = 64
SWEEPS = 4
STEPS = 2
LANES = 128
VMEM_BYTES = 40 * 1024 * 1024


def extended(x, sides, width):
    for axis, dim in sides:
        devices, length = (lax.axis_size(axis), x.shape[dim])
        up = [(i, (i + 1) % devices) for i in range(devices - 1)]
        down = [(j, i) for i, j in up]
        last = lax.slice_in_dim(x, length - width, length, axis=dim)
        leading = lax.slice_in_dim(x, 0, width, axis=dim)
        before = lax.ppermute(last, axis, up)
        after = lax.ppermute(leading, axis, down)
        x = jnp.concatenate([before, x, after], axis=dim)
    return x


def stencil_sum(framed):
    total = framed[2:, 1:-1, 1:-1] + framed[:-2, 1:-1, 1:-1]
    total = total + framed[1:-1, 2:, 1:-1] + framed[1:-1, :-2, 1:-1]
    return total + framed[1:-1, 1:-1, 2:] + framed[1:-1, 1:-1, :-2]


def two_parts(x):
    high = x.astype(jnp.bfloat16)
    low = (x - high.astype(jnp.float32)).astype(jnp.bfloat16)
    return high, low


def dot32(a, b):
    return jnp.dot(a, b, preferred_element_type=jnp.float32)


def onehot_of(hit):
    return jnp.where(hit, 1.0, 0.0).astype(jnp.bfloat16)


def gather_kernel(volt_ref, cols_ref, out_ref, parts_ref):
    cells, nodes = volt_ref.shape
    rows = out_ref.shape[0]

    @pl.when(pl.program_id(0) == 0)
    def _():
        high, low = two_parts(volt_ref[...])
        parts_ref[0:cells, :] = high
        parts_ref[cells : 2 * cells, :] = low

    lane = lax.broadcasted_iota(jnp.int32, (rows, LANES), 1)
    cell_lane = lax.broadcasted_iota(jnp.int32, (rows, cells), 1)

    def pick(cell, spot):
        hit = onehot_of(cell_lane == cell)
        wide = dot32(jnp.concatenate([hit, hit], axis=1), parts_ref[...])
        pair = lax.shift_right_arithmetic(spot, 1)
        picked = jnp.zeros((rows, LANES), jnp.float32)
        for g in range(nodes // LANES):
            picked = jnp.where(pair == g, wide[:, g * LANES : (g + 1) * LANES], picked)
        return picked

    cols = cols_ref[...]
    spot_a, spot_b = cols[:, 1:2], cols[:, 3:4]
    a = pick(cols[:, 0:1], spot_a)
    b = pick(cols[:, 2:3], spot_b)
    a = jnp.where((spot_a & 1) == 1, pltpu.roll(a, BLOCK, 1), a)
    b = jnp.where((spot_b & 1) == 0, pltpu.roll(b, BLOCK, 1), b)
    out_ref[...] = jnp.where(lane < BLOCK, a, b)


def steklov_kernel(ident_ref, volt_ref, recov_ref, template_ref, out_ref):
    index = pl.program_id(0)
    volt = volt_ref[...]

    @pl.when(index == 0)
    def _():
        out_ref[...] = -(volt - volt * volt * volt / 3.0 - recov_ref[...])

    masked = jnp.where(ident_ref[...] == index, volt, 0.0).astype(jnp.bfloat16)
    out_ref[...] += dot32(masked, template_ref[0])


def scatter_kernel(
    got_ref, sent_ref, cols_ref, conduct_ref, cells_ref, base_ref, memb_ref, memb_t_ref, current_ref, deposit_ref, gap_ref
):
    cells, nodes = base_ref.shape
    rows = got_ref.shape[0]

    @pl.when(pl.program_id(0) == 0)
    def _():
        gap_ref[...] = jnp.zeros_like(gap_ref)

    lane = lax.broadcasted_iota(jnp.int32, (rows, LANES), 1)
    half = jnp.where(lane < BLOCK, 0, 1)
    cols = cols_ref[...]
    conduct = conduct_ref[...]
    scale = jnp.where(lane < BLOCK, conduct[:, 0:1], conduct[:, 1:2])
    flux = scale * (got_ref[...] - pltpu.roll(sent_ref[...], BLOCK, 1))
    turned = pltpu.roll(flux, BLOCK, 1)
    own_row = lax.broadcasted_iota(jnp.int32, (cells, rows), 0)

    def spread(cell_row, spot, home):
        hit = onehot_of(own_row == cell_row)
        side = spot & 1
        placed = jnp.where(half == side, jnp.where(side == home, flux, turned), 0.0)
        pair = lax.shift_right_arithmetic(spot, 1)
        total = []
        for g in range(nodes // LANES):
            high, low = two_parts(jnp.where(pair == g, placed, 0.0))
            total.append(jnp.concatenate([high, low], axis=0))
        return dot32(jnp.concatenate([hit, hit], axis=1), jnp.concatenate(total, axis=1))

    gap_ref[...] += spread(cells_ref[1:2, :], cols[:, 3:4], 0)
    gap_ref[...] += spread(cells_ref[0:1, :], cols[:, 1:2], 1)

    @pl.when(pl.program_id(0) == pl.num_programs(0) - 1)
    def _():
        current = base_ref[...] - gap_ref[...]
        current_ref[...] = current
        grid_rows = deposit_ref.shape[0]
        grid_row = lax.broadcasted_iota(jnp.int32, (grid_rows, cells), 0)
        cell_lane = lax.broadcasted_iota(jnp.int32, (cells, LANES), 1)
        total = jnp.zeros(deposit_ref.shape, jnp.float32)
        for k in range(nodes // BLOCK):
            g = k // 2
            part = current[:, g * LANES : (g + 1) * LANES]
            kept = (cell_lane < BLOCK) if k % 2 == 0 else (cell_lane >= BLOCK)
            mean = jnp.sum(jnp.where(kept, part, 0.0), axis=1, keepdims=True) * (1.0 / BLOCK)
            column = memb_ref[:, k : k + 1] & (LANES - 1)
            high, low = two_parts(jnp.where(cell_lane == column, mean, 0.0))
            hit = onehot_of(grid_row == lax.shift_right_arithmetic(memb_t_ref[k : k + 1, :], 7))
            total = total + dot32(hit, high) + dot32(hit, low)
        deposit_ref[...] = total


def update_kernel(volt_ref, recov_ref, current_ref, phi_ref, memb_ref, volt_out, recov_out):
    cells, nodes = volt_ref.shape
    grid_rows = phi_ref.shape[0]
    high, low = two_parts(phi_ref[...])
    both = jnp.concatenate([high, low], axis=0)
    lane = lax.broadcasted_iota(jnp.int32, (cells, LANES), 1)
    grid_lane = lax.broadcasted_iota(jnp.int32, (cells, grid_rows), 1)

    def value(k):
        memb = memb_ref[:, k : k + 1]
        hit = onehot_of(grid_lane == lax.shift_right_arithmetic(memb, 7))
        row = dot32(jnp.concatenate([hit, hit], axis=1), both)
        return jnp.sum(jnp.where(lane == (memb & (LANES - 1)), row, 0.0), axis=1, keepdims=True)

    for g in range(nodes // LANES):
        phi_nodes = jnp.where(lane < BLOCK, value(2 * g), value(2 * g + 1))
        span = slice(g * LANES, (g + 1) * LANES)
        volt, recov = volt_ref[:, span], recov_ref[:, span]
        recov_out[:, span] = recov + 0.05 * 0.08 * (volt + 0.7 - 0.8 * recov)
        volt_out[:, span] = volt - 0.05 * (current_ref[:, span] + phi_nodes)


def params():
    return pltpu.CompilerParams(vmem_limit_bytes=VMEM_BYTES)


def whole_block(shape):
    return pl.BlockSpec(shape, lambda i: (0,) * len(shape))


def gather(volt, cols, slots, tile):
    cells, nodes = volt.shape
    return pl.pallas_call(
        gather_kernel,
        grid=(slots // tile,),
        in_specs=[whole_block((cells, nodes)), pl.BlockSpec((tile, 4), lambda i: (i, 0))],
        out_specs=pl.BlockSpec((tile, LANES), lambda i: (i, 0)),
        out_shape=jax.ShapeDtypeStruct((slots, LANES), jnp.float32),
        scratch_shapes=[pltpu.VMEM((2 * cells, nodes), jnp.bfloat16)],
        compiler_params=params(),
    )(volt, cols)


def steklov(ident, volt, recov, templates):
    cells, nodes = volt.shape
    count = templates.shape[0]
    return pl.pallas_call(
        steklov_kernel,
        grid=(count,),
        in_specs=[
            whole_block((cells, 1)),
            whole_block((cells, nodes)),
            whole_block((cells, nodes)),
            pl.BlockSpec((1, nodes, nodes), lambda i: (i, 0, 0)),
        ],
        out_specs=whole_block((cells, nodes)),
        out_shape=jax.ShapeDtypeStruct((cells, nodes), jnp.float32),
        compiler_params=params(),
        cost_estimate=pl.CostEstimate(
            flops=2 * count * cells * nodes * nodes, bytes_accessed=2 * count * nodes * nodes, transcendentals=0
        ),
    )(ident, volt, recov, templates)


def scatter(got, sent, cols, conduct, cell_rows, base, memb, memb_t, grid_rows, tile):
    cells, nodes = base.shape
    slots = got.shape[0]
    return pl.pallas_call(
        scatter_kernel,
        grid=(slots // tile,),
        in_specs=[
            pl.BlockSpec((tile, LANES), lambda i: (i, 0)),
            pl.BlockSpec((tile, LANES), lambda i: (i, 0)),
            pl.BlockSpec((tile, 4), lambda i: (i, 0)),
            pl.BlockSpec((tile, 2), lambda i: (i, 0)),
            pl.BlockSpec((2, tile), lambda i: (0, i)),
            whole_block((cells, nodes)),
            whole_block(memb.shape),
            whole_block(memb_t.shape),
        ],
        out_specs=[whole_block((cells, nodes)), whole_block((grid_rows, LANES))],
        out_shape=[
            jax.ShapeDtypeStruct((cells, nodes), jnp.float32),
            jax.ShapeDtypeStruct((grid_rows, LANES), jnp.float32),
        ],
        scratch_shapes=[pltpu.VMEM((cells, nodes), jnp.float32)],
        compiler_params=params(),
    )(got, sent, cols, conduct, cell_rows, base, memb, memb_t)


def update(volt, recov, current, phi, memb):
    return pl.pallas_call(
        update_kernel,
        out_shape=[jax.ShapeDtypeStruct(volt.shape, jnp.float32)] * 2,
        compiler_params=params(),
    )(volt, recov, current, phi, memb)


def slot_table(patch_src, targets, patch_dst, patch_conduct, devices, capacity):
    patches = patch_src.shape[0]
    onehot = (targets[:, None] == jnp.arange(devices, dtype=jnp.int32)[None, :]).astype(jnp.int32)
    order = jnp.arange(patches, dtype=jnp.int32)
    earlier = (order[:, None] > order[None, :]).astype(jnp.bfloat16)
    before = dot32(earlier, onehot.astype(jnp.bfloat16))
    slot = jnp.sum(onehot * before.astype(jnp.int32), axis=1)
    position = targets * capacity + slot
    hit = (jnp.arange(devices * capacity, dtype=jnp.int32)[:, None] == position[None, :]).astype(jnp.bfloat16)
    first = lax.reduce_precision(patch_conduct, 8, 7)
    second = lax.reduce_precision(patch_conduct - first, 8, 7)
    third = patch_conduct - first - second
    values = [patch_src // BLOCK, patch_src % BLOCK, patch_dst // BLOCK, patch_dst % BLOCK]
    values = [v.astype(jnp.bfloat16) for v in values + [jnp.ones_like(patch_src), first, second, third]]
    table = dot32(hit, jnp.stack(values, axis=1))
    empty = table[:, 4] - 1.0
    src = table[:, 0] * BLOCK + table[:, 1] + empty
    dst = table[:, 2] * BLOCK + table[:, 3] + empty
    return src, dst, table[:, 5] + table[:, 6] + table[:, 7]


def exchange(x):
    return lax.all_to_all(x, ("tx", "ty"), split_axis=0, concat_axis=0, tiled=True)


def on_device(
    potential,
    gating,
    ecs_start,
    templates,
    template_id,
    patch_src,
    patch_dev,
    patch_dst,
    patch_conduct,
    memb_point,
):
    cells, nodes = potential.shape
    per_cell = nodes // BLOCK
    tile = ecs_start.shape[0]
    points = ecs_start.size
    count_x = lax.axis_size("tx")
    count_y = lax.axis_size("ty")
    devices = count_x * count_y
    patches = patch_src.shape[0]
    capacity = 2 * patches // devices
    slots = devices * capacity
    rows_at_once = min(512, slots)
    src, dst, conduct = slot_table(patch_src, patch_dev[:, 0], patch_dst, patch_conduct, devices, capacity)
    head = jnp.concatenate([dst.reshape(devices, capacity), conduct.reshape(devices, capacity)], axis=1)
    got_head = exchange(head)
    got_dst = got_head[:, :capacity].reshape(slots)
    got_conduct = got_head[:, capacity:].reshape(slots)
    places = []
    for patch in (src, got_dst):
        patch = patch.astype(jnp.int32)
        places += [jnp.where(patch < 0, -1, patch // per_cell), patch % per_cell]
    cols = jnp.stack(places, axis=1)
    cell_rows = jnp.stack([places[0], places[2]], axis=0)
    conduct_cols = jnp.stack([got_conduct, conduct], axis=1)
    memb = memb_point.reshape(cells, per_cell)
    memb_t = memb.T
    ident = template_id[:, None]
    start_x = lax.axis_index("tx") * tile
    start_y = lax.axis_index("ty") * tile
    volt = potential
    recov = gating
    phi = ecs_start
    for step in range(STEPS):
        sent = gather(volt, cols, slots, rows_at_once)
        got = exchange(sent.reshape(devices, capacity, LANES)).reshape(slots, LANES)
        base = steklov(ident, volt, recov, templates)
        depth = SWEEPS
        framed_phi = extended(phi, (("tx", 0), ("ty", 1)), depth)
        got, framed_phi = lax.optimization_barrier((got, framed_phi))
        current, deposit = scatter(
            got, sent, cols, conduct_cols, cell_rows, base, memb, memb_t, points // LANES, rows_at_once
        )
        deposit = deposit.reshape(ecs_start.shape)
        framed_dep = extended(deposit, (("tx", 0), ("ty", 1)), depth)
        current_phi = framed_phi
        for sweep in range(SWEEPS):
            rim = depth - sweep - 1
            padded = jnp.pad(current_phi, ((0, 0), (0, 0), (1, 1)))
            total = stencil_sum(padded)
            lo = depth - rim
            hi = depth + tile + rim
            dep_crop = framed_dep[lo:hi, lo:hi, :]
            updated = (dep_crop + total) / 6.5
            span = jnp.arange(tile + 2 * rim, dtype=jnp.int32) - rim
            inside_x = (start_x + span >= 0) & (start_x + span < tile * count_x)
            inside_y = (start_y + span >= 0) & (start_y + span < tile * count_y)
            inside = inside_x[:, None, None] & inside_y[None, :, None]
            current_phi = jnp.where(inside, updated, 0.0)
        phi = current_phi
        volt, recov = update(volt, recov, current, phi.reshape(points // LANES, LANES), memb)
    return (volt, phi)


def solution(mesh):
    return jax.shard_map(
        on_device,
        mesh=mesh,
        in_specs=(
            P(("tx", "ty"), None),
            P(("tx", "ty"), None),
            P("tx", "ty", None),
            P(),
            P(("tx", "ty")),
            P(("tx", "ty")),
            P(("tx", "ty"), None),
            P(("tx", "ty")),
            P(("tx", "ty")),
            P(("tx", "ty")),
        ),
        out_specs=(P(("tx", "ty"), None), P("tx", "ty", None)),
        check_vma=False,
    )
```
